32 devices in a mesh: groups: 2 (over y), inst: 8 (over z, x), tensor: 2 (over core).
Axes of the slice: x: 2, y: 2, z: 4, core: 2. Of those that a mesh axis runs over, the one named last changes fastest.
Arguments:
- hidden: bfloat16 [2048, 2560], P(('groups', 'inst'), 'tensor'), parts along dimension 0, may hold values from -6 to 6
- value_weight: bfloat16 [2560, 512], P('tensor'), may hold values from -0.125 to 0.125
- adapter_down: bfloat16 [1024, 2560], P(('groups', 'inst', 'tensor')), parts along dimension 0, may hold values from -0.125 to 0.125
- adapter_up: bfloat16 [1024, 512], P(('groups', 'inst', 'tensor')), parts along dimension 0, may hold values from -0.75 to 0.75
- block_adapter: int32 [16], P('groups'), parts along dimension 0, may hold values from 0 to 7
- queries: bfloat16 [2048, 4096], P(('groups', 'inst'), 'tensor'), parts along dimension 0, may hold values from -65 to 65
- new_keys: bfloat16 [2048, 512], P(('groups', 'inst'), 'tensor'), parts along dimension 0, may hold values from -5 to 5
- kv_pool: bfloat16 [3072, 16, 1024], P(('groups', 'inst'), None, 'tensor'), parts along dimension 0, may hold values from -6 to 6
- page_request: int32 [3072], P(('groups', 'inst')), parts along dimension 0, may hold values from -1 to 7
- page_pos: int32 [3072], P(('groups', 'inst')), parts along dimension 0, may hold values from 0 to 255
- token_request: int32 [2048], P(('groups', 'inst')), parts along dimension 0, may hold values from 0 to 7
- token_pos: int32 [2048], P(('groups', 'inst')), parts along dimension 0, may hold values from 0 to 4095
- send_page: int32 [96], P(('groups', 'inst')), parts along dimension 0, may hold values from 0 to 191, as said below
- send_dest: int32 [96], P(('groups', 'inst')), parts along dimension 0, may hold values from 0 to 7, as said below
- dest_slot: int32 [96], P(('groups', 'inst')), parts along dimension 0, may hold values from 0 to 191, as said below
- send_count: int32 [16], P(('groups', 'inst')), parts along dimension 0, may hold values from 3 to 6, as said below
Outputs:
- attended: bfloat16 [2048, 4096], P(('groups', 'inst'), 'tensor'), parts along dimension 0
- new_values: bfloat16 [2048, 512], P(('groups', 'inst'), 'tensor'), parts along dimension 0
The draws below stay inside these ranges and needn't reach their ends.
There are 2 independent parts, one for each index of `groups`. The reference program is written for one: setup_inputs(seed, part) draws one part's arguments, and reference() takes and returns one part's arrays. A program takes and returns all parts, laid end to end along the dimension named above; an argument that names none is the same for every part. Nothing has to cross between parts.
Inputs may be any that keep to these rules, and one draw needn't show every extreme that they name: Page slots of one instance in send_page are distinct, and differ from all slots named for that instance in dest_slot. `send_dest`: the entries of one instance name 6 different instances other than itself, and every instance is named by exactly one entry of each position k of the lists. `dest_slot`: no receiver slot is named twice. `send_count`: some instance has 6 live entries.
All inputs are finite; a program needn't handle non-finite values.
Results may differ from the reference program's by a relative error of at most 0.0043.
Values may be sent and summed in bfloat16 or wider, within the bound.
A program may use at most 128 MiB of HBM per device.

```python
import math
import jax
import jax.numpy as jnp
import numpy as np
from jax import lax

D = 2560
QH = 32
KVH = 4
HD = 128
R = 64
LBLOCK = 128
TOK = 128
BLOCKS = 1
PAGE = 16
PAGES = 192
REQ = 8
CTX_PAGES = 256
MIG = 6
NADP = 8
TOKENS = 1024
N_INST = 8


def migration_plan(key):
    k_order, k_offset, k_slots, k_count, k_first, k_second = jax.random.split(key, 6)
    order = jax.random.permutation(k_order, N_INST).astype(jnp.int32)
    inverse = jnp.argsort(order).astype(jnp.int32)
    offsets = (1 + jax.random.permutation(k_offset, N_INST - 1)[:MIG]).astype(jnp.int32)
    targets = order[(inverse[:, None] + offsets[None, :]) % N_INST]
    slot_keys = jax.random.split(k_slots, N_INST)
    slots = jax.vmap(lambda k: jax.random.permutation(k, PAGES))(slot_keys).astype(jnp.int32)
    sending = slots[:, :MIG]
    receiving = slots[:, MIG:2 * MIG]
    position = jnp.arange(MIG, dtype=jnp.int32)
    landing = receiving[targets, position[None, :]]
    counts = jax.random.randint(k_count, (N_INST,), MIG // 2, MIG + 1).astype(jnp.int32)
    first = jax.random.randint(k_first, (), 0, N_INST)
    second = (first + 1 + jax.random.randint(k_second, (), 0, N_INST - 1)) % N_INST
    counts = counts.at[first].set(MIG).at[second].set(MIG // 2)
    senders = order[(inverse[:, None] - offsets[None, :]) % N_INST]
    arriving = position[None, :] < counts[senders]
    leaving = position[None, :] < counts[:, None]
    return (targets, sending, landing, counts, receiving, arriving, leaving)


def draw_send_page(key, part):
    plan = migration_plan(key)
    return plan[1].reshape(-1)


def draw_send_dest(key, part):
    plan = migration_plan(key)
    return plan[0].reshape(-1)


def draw_dest_slot(key, part):
    plan = migration_plan(key)
    return plan[2].reshape(-1)


def draw_send_count(key, part):
    plan = migration_plan(key)
    return plan[3]


def draw_page_request(key, part):
    targets, sending, landing, counts, receiving, arriving, leaving = migration_plan(key)
    key = jax.random.fold_in(key, 11)
    owners = jax.random.randint(key, (N_INST, PAGES), 0, REQ).astype(jnp.int32)
    rows = jnp.arange(N_INST, dtype=jnp.int32)[:, None]
    owners = owners.at[rows, sending].set(jnp.where(leaving, -1, owners[rows, sending]))
    owners = owners.at[rows, receiving].set(jnp.where(arriving, owners[rows, receiving], -1))
    return owners.reshape(-1)


def token_keys(key):
    return jnp.clip(jax.random.normal(key, (TOKENS, KVH * HD), jnp.float32), -5.0, 5.0).astype(jnp.bfloat16)


def draw_new_keys(key, part):
    return token_keys(key)


def draw_queries(key, part):
    key = jax.random.fold_in(key, 5)
    drawn = jnp.clip(jax.random.normal(key, (TOKENS, QH * HD), jnp.float32), -5.0, 5.0)
    return drawn.astype(jnp.bfloat16)


def touch_ends(array, own_key, smallest, largest):
    spot = [jax.random.randint(jax.random.fold_in(own_key, axis), (), 0, length) for axis, length in enumerate(array.shape)]
    longest = array.shape.index(max(array.shape))
    beside = spot[:longest] + [(spot[longest] + 1) % array.shape[longest]] + spot[longest + 1:]
    return array.at[tuple(spot)].set(smallest).at[tuple(beside)].set(largest)


def block_levels(rng, dims, pieces, low, high):
    level = 1.0
    for axis_at, shards_of in pieces:
        steps = jax.random.uniform(jax.random.fold_in(jax.random.fold_in(rng, 6), axis_at), (shards_of,), jnp.float32, low / len(pieces), high / len(pieces))
        level = level * jnp.repeat(jnp.exp(steps), dims[axis_at] // shards_of).reshape((-1,) + (1,) * (len(dims) - 1 - axis_at))
    return level


def rank_bounds(number_of, lean):
    loads = [(1 << 20) // math.isqrt(rank ** lean) + 1 for rank in range(1, number_of + 1)]
    width = 1 + sum(loads) // (1 << 30)
    return np.cumsum(np.array([max(1, weight // width) for weight in loads]))


def ranked(own_key, dims, number_of, lean):
    table = rank_bounds(number_of, lean)
    ticket = jax.random.randint(jax.random.fold_in(own_key, 1), dims, 0, int(table[number_of - 1]))
    standing = jnp.searchsorted(jnp.asarray(table, jnp.int32), ticket, side="right")
    return jax.random.permutation(jax.random.fold_in(own_key, 2), number_of)[standing].astype(jnp.int32)


def noise(own_key, extent, spread, reach, shards=(), kind=jnp.bfloat16):
    result = jax.random.normal(own_key, extent, jnp.float32) * spread
    if len(shards) > 0:
        result = block_levels(own_key, extent, shards, -0.22, 0.18) * result
    return jnp.clip(result, min=-reach, max=reach).astype(kind)


def setup_inputs(seed: int = 0, part: int = 0) -> dict:
    splits = jax.random.split(jax.random.key(seed), 17)
    part_splits = jax.random.split(jax.random.fold_in(splits[16], part), 17)
    hidden = noise(part_splits[0], (TOKENS, D), 1.0, 6.0, ((0, 8), (1, 2)))
    value_weight = noise(splits[1], (D, KVH * HD), D ** -0.5, 0.125, ((0, 2),))
    adapter_down = noise(part_splits[2], (NADP * R, D), D ** -0.5, 0.125, ((0, 16),))
    adapter_up = noise(part_splits[3], (NADP * R, KVH * HD), R ** -0.5, 0.75, ((0, 16),))
    block_adapter = touch_ends(ranked(part_splits[4], (N_INST * BLOCKS,), NADP, 2), jax.random.fold_in(part_splits[4], 3), 0, NADP - 1).astype(jnp.int32)
    queries = draw_queries(jax.random.fold_in(jax.random.fold_in(splits[16], part), 71), part)
    new_keys = draw_new_keys(jax.random.fold_in(jax.random.fold_in(splits[16], part), 71), part)
    kv_pool = noise(part_splits[7], (N_INST * PAGES, PAGE, KVH * 2 * HD), 1.0, 6.0, ((0, 8), (2, 2)))
    page_request = draw_page_request(jax.random.fold_in(jax.random.fold_in(splits[16], part), 71), part)
    page_pos = touch_ends(jax.random.randint(part_splits[9], (N_INST * PAGES,), 0, CTX_PAGES), jax.random.fold_in(part_splits[9], 1), 0, CTX_PAGES - 1).astype(jnp.int32)
    token_request = touch_ends(jax.random.randint(part_splits[10], (TOKENS,), 0, REQ), jax.random.fold_in(part_splits[10], 1), 0, REQ - 1).astype(jnp.int32)
    token_pos = touch_ends(jax.random.randint(part_splits[11], (TOKENS,), 0, CTX_PAGES * PAGE), jax.random.fold_in(part_splits[11], 1), 0, (CTX_PAGES * PAGE) - 1).astype(jnp.int32)
    send_page = draw_send_page(jax.random.fold_in(jax.random.fold_in(splits[16], part), 71), part)
    send_dest = draw_send_dest(jax.random.fold_in(jax.random.fold_in(splits[16], part), 71), part)
    dest_slot = draw_dest_slot(jax.random.fold_in(jax.random.fold_in(splits[16], part), 71), part)
    send_count = draw_send_count(jax.random.fold_in(jax.random.fold_in(splits[16], part), 71), part)
    return {"hidden": hidden, "value_weight": value_weight, "adapter_down": adapter_down, "adapter_up": adapter_up, "block_adapter": block_adapter, "queries": queries, "new_keys": new_keys, "kv_pool": kv_pool, "page_request": page_request, "page_pos": page_pos, "token_request": token_request, "token_pos": token_pos, "send_page": send_page, "send_dest": send_dest, "dest_slot": dest_slot, "send_count": send_count}


def reference(hidden, value_weight, adapter_down, adapter_up, block_adapter, queries, new_keys, kv_pool, page_request, page_pos, token_request, token_pos, send_page, send_dest, dest_slot, send_count):
    kv_cols = KVH * HD
    highest = lax.Precision.HIGHEST
    base = jnp.dot(hidden, value_weight, preferred_element_type=jnp.float32)
    downs = adapter_down.reshape(NADP, R, D)[block_adapter]
    ups = adapter_up.reshape(NADP, R, kv_cols)[block_adapter]
    token_blocks = hidden.reshape(N_INST * BLOCKS, LBLOCK, D)
    low = jnp.einsum('bnd,brd->bnr', token_blocks.astype(jnp.float32), downs.astype(jnp.float32), precision=highest)
    delta = jnp.einsum('bnr,brk->bnk', low, ups.astype(jnp.float32), precision=highest)
    new_values = (base + delta.reshape(TOKENS, kv_cols)).astype(jnp.bfloat16)
    entry = jnp.arange(N_INST * MIG, dtype=jnp.int32)
    source = entry // MIG
    live = entry % MIG < send_count[source]
    src_row = source * PAGES + send_page
    dst_row = jnp.where(live, send_dest * PAGES + dest_slot, N_INST * PAGES).astype(jnp.int32)
    pool = kv_pool.at[dst_row].set(kv_pool[src_row], mode='drop')
    page_tokens = (page_pos[:, None] * PAGE + jnp.arange(PAGE, dtype=jnp.int32)[None, :]).reshape(N_INST, PAGES * PAGE)
    page_owner = jnp.repeat(page_request, PAGE).reshape(N_INST, PAGES * PAGE)
    scale = 1.0 / math.sqrt(HD)

    def one_instance(items):
        query, key_new, value_new, pool_here, owner, key_pos, t_req, t_pos = items
        keys = jnp.concatenate([pool_here[:, :, 0, :], key_new], axis=0).astype(jnp.float32)
        values = jnp.concatenate([pool_here[:, :, 1, :], value_new], axis=0).astype(jnp.float32)
        key_req = jnp.concatenate([owner, t_req], axis=0)
        key_at = jnp.concatenate([key_pos, t_pos], axis=0)
        grouped = query.reshape(TOK, KVH, QH // KVH, HD).astype(jnp.float32)
        scores = jnp.einsum('tghd,lgd->tghl', grouped, keys, precision=highest) * scale
        valid = (key_req[None, :] == t_req[:, None]) & (key_at[None, :] <= t_pos[:, None])
        valid = valid[:, None, None, :]
        top = lax.optimization_barrier(jnp.max(jnp.where(valid, scores, -jnp.inf), axis=-1, keepdims=True))
        raised = jnp.where(valid, jnp.exp(scores - top), 0.0)
        probs = (raised / lax.optimization_barrier(jnp.sum(raised, axis=-1, keepdims=True))).astype(jnp.bfloat16)
        out = jnp.einsum('tghl,lgd->tghd', probs.astype(jnp.float32), values, precision=highest)
        return out.reshape(TOK, QH * HD).astype(jnp.bfloat16)
    attended = lax.map(one_instance, (queries.reshape(N_INST, TOK, QH * HD), new_keys.reshape(N_INST, TOK, KVH, HD), new_values.reshape(N_INST, TOK, KVH, HD), pool.reshape(N_INST, PAGES * PAGE, KVH, 2, HD), page_owner, page_tokens, token_request.reshape(N_INST, TOK), token_pos.reshape(N_INST, TOK)))
    return (attended.reshape(TOKENS, QH * HD), new_values)
```

```python
import functools
import math

import jax
import jax.numpy as jnp
from jax import lax
from jax.experimental import pallas as pl
from jax.experimental.pallas import tpu as pltpu
from jax.sharding import PartitionSpec as P

HD = 128
FAR = -1e30
F32 = jnp.float32
BF16 = jnp.bfloat16
MESH = pl.DeviceIdType.MESH


def dot(a, b):
    return jnp.dot(a, b, preferred_element_type=F32)


def dot_t(a, b):
    return lax.dot_general(a, b, (((1,), (1,)), ((), ())), preferred_element_type=F32)


def kernel(
    inst,
    block_adapter,
    send_page,
    send_dest,
    dest_slot,
    send_count,
    page_info,
    token_info,
    hidden,
    weight,
    down,
    up,
    queries,
    new_keys,
    pool,
    attended,
    new_values,
    stage1,
    recv1,
    stage2,
    recv2,
    out_pages,
    in_pages,
    out_slots,
    in_slots,
    hid_other,
    down_f,
    up_f,
    combined,
    recvc,
    q3,
    vaug,
    bias,
    bias2,
    k2,
    v2,
    acc,
    top,
    one_send,
    one_recv,
    two_send,
    two_recv,
    page_send,
    page_recv,
    slot_send,
    slot_recv,
    pair_send,
    pair_recv,
):
    me = lax.axis_index("inst")
    t = lax.axis_index("tensor")
    other = 1 - t
    tokens = hidden.shape[0]
    feats = hidden.shape[1]
    rank = down.shape[0]
    pages, page_tokens, _ = pool.shape
    keys = pages * page_tokens
    heads = q3.shape[0]
    groups = new_keys.shape[1] // HD
    per = heads // groups
    vals = groups * HD
    mig = send_page.shape[0]
    slots = stage1.shape[1] // 16
    c = math.log2(math.e) / math.sqrt(HD)

    def peer(o):
        return lax.rem(me + o, inst)

    def source(o):
        return lax.rem(me - o + inst, inst)

    def each(body):
        lax.fori_loop(1, inst, lambda o, _: (body(o), 0)[1], 0)

    barrier = pltpu.get_barrier_semaphore()
    each(
        lambda o: pl.semaphore_signal(
            barrier, inc=1, device_id={"inst": peer(o)}, device_id_type=MESH
        )
    )
    pl.semaphore_signal(barrier, inc=1, device_id={"tensor": other}, device_id_type=MESH)

    def remote(src, dst, send, recv, o):
        return pltpu.make_async_remote_copy(
            src_ref=src,
            dst_ref=dst,
            send_sem=send.at[o],
            recv_sem=recv.at[o],
            device_id={"inst": peer(o)},
            device_id_type=MESH,
        )

    def paired(src, dst, k):
        return pltpu.make_async_remote_copy(
            src_ref=src,
            dst_ref=dst,
            send_sem=pair_send.at[k],
            recv_sem=pair_recv.at[k],
            device_id={"tensor": other},
            device_id_type=MESH,
        )

    slot_copy = lambda o: remote(out_slots.at[peer(o)], in_slots.at[me], slot_send, slot_recv, o)
    slot_in = lambda o: remote(
        out_slots.at[peer(o)], in_slots.at[source(o)], slot_send, slot_recv, o
    )
    page_copy = lambda o: remote(out_pages.at[peer(o)], in_pages.at[me], page_send, page_recv, o)
    page_in = lambda o: remote(
        out_pages.at[peer(o)], in_pages.at[source(o)], page_send, page_recv, o
    )
    one_copy = lambda o: remote(stage1.at[peer(o)], recv1.at[me], one_send, one_recv, o)
    one_in = lambda o: remote(stage1.at[peer(o)], recv1.at[source(o)], one_send, one_recv, o)
    two_copy = lambda o: remote(stage2.at[peer(o)], recv2.at[me], two_send, two_recv, o)
    two_in = lambda o: remote(stage2.at[peer(o)], recv2.at[source(o)], two_send, two_recv, o)

    cols = down.shape[1] // HD
    tiles = []
    for h in range(rank // 16):
        for k in range(cols):
            tiles.append((down, h, k))
    for h in range(rank // 16):
        for k in range(up.shape[1] // HD):
            tiles.append((up, h, k))
    for q, (ref, h, k) in enumerate(tiles):
        at = (q % slots) * 16
        stage1[q // slots, at : at + 16, :] = ref[h * 16 : h * 16 + 16, k * HD : (k + 1) * HD]
    for q in range(len(tiles), inst * slots):
        at = (q % slots) * 16
        stage1[q // slots, at : at + 16, :] = jnp.zeros((16, HD), BF16)

    count = send_count[0]

    def choose(j, _):
        def look(k, found):
            page, slot = found
            hit = (send_dest[k] == j) & (k < count)
            return jnp.where(hit, send_page[k], page), jnp.where(hit, dest_slot[k], slot)

        page, slot = lax.fori_loop(
            0, mig, look, (jnp.int32(0), jnp.int32(-1)), unroll=mig <= 8
        )
        out_slots[j] = jnp.full(out_slots.shape[1:], slot, jnp.int32)
        out_pages[j] = pool[page]
        return 0

    lax.fori_loop(0, inst, choose, 0)

    pl.semaphore_wait(barrier, inst)
    each(lambda o: slot_copy(o).start())
    each(lambda o: one_copy(o).start())
    paired(hidden, hid_other, 0).start()
    each(lambda o: page_copy(o).start())
    recv1[me] = stage1[me]
    in_slots[me] = jnp.full(in_slots.shape[1:], -1, jnp.int32)
    in_pages[me] = jnp.zeros(in_pages.shape[1:], BF16)

    base = dot(hidden[...], weight[...])
    for h in range(2):
        combined[h] = base[:, h * vals : (h + 1) * vals]
    for h in range(heads):
        q3[h] = queries[:, h * HD : (h + 1) * HD]
    for g in range(groups):
        vaug[g, :, :HD] = pool[:, :, (2 * g + 1) * HD : (2 * g + 2) * HD].reshape(keys, HD)
        vaug[g, :, HD:] = jnp.ones((keys, HD), BF16)
        v2[g, :, HD:] = jnp.ones((v2.shape[1], HD), BF16)

    t_row = token_info[...].astype(F32)
    t_req = jnp.broadcast_to(t_row[0:1], (tokens, tokens)).T[:, 0:1]
    t_pos = jnp.broadcast_to(t_row[1:2], (tokens, tokens)).T[:, 0:1]

    each(lambda o: slot_in(o).wait_recv())
    lane = lax.broadcasted_iota(jnp.int32, (1, HD), 1)
    info = page_info[...].astype(F32)
    page_col = lax.broadcasted_iota(jnp.int32, (pages, HD), 0)
    gone = jnp.zeros((8, pages), F32)
    per_row = HD // page_tokens
    for b in range(inst // per_row):
        row = jnp.full((1, HD), -1, jnp.int32)
        for j in range(per_row):
            row = jnp.where(lane // page_tokens == j, in_slots[b * per_row + j][0:1], row)
        match = (page_col == row).astype(F32).astype(BF16)
        gone = gone + dot_t(jnp.ones((8, HD), BF16), match)
        found = dot(info.astype(BF16), match)
        req = jnp.where(row >= 0, found[0:1], -2.0)
        at = found[1:2] * page_tokens + (lane % page_tokens).astype(F32)
        ok = (req == t_req) & (at <= t_pos)
        bias2[:, b * HD : (b + 1) * HD] = jnp.where(ok, 0.0, FAR)
    ok = (t_row[0:1] == t_req) & (t_row[1:2] <= t_pos)
    bias2[:, inst * page_tokens :] = jnp.where(ok, 0.0, FAR)
    first = lax.broadcasted_iota(jnp.int32, (8, pages), 0) == 0
    info = jnp.where(first & (gone > 0.5), -1.0, info).astype(BF16)
    spread_page = lax.broadcasted_iota(jnp.int32, (pages, keys), 0)
    spread_key = lax.broadcasted_iota(jnp.int32, (pages, keys), 1) // page_tokens
    spread = (spread_page == spread_key).astype(F32).astype(BF16)
    key_info = dot(info, spread)
    entry = lax.broadcasted_iota(jnp.int32, (1, keys), 1) % page_tokens
    key_at = key_info[1:2] * page_tokens + entry.astype(F32)
    ok = (key_info[0:1] == t_req) & (key_at <= t_pos)
    bias[...] = jnp.where(ok, 0.0, FAR)

    each(lambda o: one_in(o).wait_recv())

    def pick(j, _):
        stage2[j] = recv1[block_adapter[j]]
        return 0

    lax.fori_loop(0, inst, pick, 0)
    each(lambda o: two_copy(o).start())
    recv2[me] = stage2[me]

    both = 2

    def pool_part(g):
        def step(i, _):
            h = g * per + i * both
            q = q3[pl.ds(h, both)].reshape(both * tokens, HD)
            k = pool[:, :, 2 * g * HD : (2 * g + 1) * HD].reshape(keys, HD)
            s = dot_t(q, k).reshape(both, tokens, keys) + bias[...][None]
            m = jnp.max(s, axis=-1, keepdims=True)
            p = jnp.exp2((s - m) * c).astype(BF16).reshape(both * tokens, keys)
            acc[pl.ds(h, both)] = dot(p, vaug[g]).reshape(both, tokens, 2 * HD)
            top[pl.ds(h, both)] = jnp.broadcast_to(m, (both, tokens, HD))
            return 0

        lax.fori_loop(0, per // both, step, 0)

    half = groups // 2
    for g in range(half):
        pool_part(g)

    each(lambda o: two_in(o).wait_recv())
    paired(hidden, hid_other, 0).wait_recv()
    for q, (ref, h, k) in enumerate(tiles):
        at = (q % slots) * 16
        tile = recv2[q // slots, at : at + 16, :]
        if ref is down:
            side, col = divmod(k * HD, feats)
            down_f[side, h * 16 : h * 16 + 16, col : col + HD] = tile
        else:
            up_f[h * 16 : h * 16 + 16, k * HD : (k + 1) * HD] = tile
    low = dot_t(hidden[...], down_f[t]) + dot_t(hid_other[...], down_f[other])
    delta = jnp.zeros((tokens, up.shape[1]), F32)
    for _ in range(3):
        part = low.astype(BF16)
        low = low - part.astype(F32)
        delta = delta + dot(part, up_f[...])
    for h in range(2):
        combined[h] = combined[h] + delta[:, h * vals : (h + 1) * vals]
    paired(combined.at[other], recvc, 1).start()

    for g in range(half, groups):
        pool_part(g)

    paired(combined.at[other], recvc, 1).wait_recv()
    each(lambda o: page_in(o).wait_recv())
    values = (combined[t] + recvc[...]).astype(BF16)
    new_values[...] = values
    arrived = inst * page_tokens
    for g in range(groups):
        k2[g, :arrived, :] = in_pages[:, :, 2 * g * HD : (2 * g + 1) * HD].reshape(arrived, HD)
        k2[g, arrived:, :] = new_keys[:, g * HD : (g + 1) * HD]
        v2[g, :arrived, :HD] = in_pages[:, :, (2 * g + 1) * HD : (2 * g + 2) * HD].reshape(
            arrived, HD
        )
        v2[g, arrived:, :HD] = values[:, g * HD : (g + 1) * HD]
    for h in range(0, heads, both):
        g = h // per
        q = q3[h : h + both].reshape(both * tokens, HD)
        s = dot_t(q, k2[g]).reshape(both, tokens, k2.shape[1]) + bias2[...][None]
        m_old = top[h : h + both][:, :, 0:1]
        m = jnp.maximum(jnp.max(s, axis=-1, keepdims=True), m_old)
        p = jnp.exp2((s - m) * c).astype(BF16).reshape(both * tokens, k2.shape[1])
        keep = jnp.exp2((m_old - m) * c)
        whole = acc[h : h + both] * keep + dot(p, v2[g]).reshape(both, tokens, 2 * HD)
        done = (whole[:, :, :HD] / whole[:, :, HD:]).astype(BF16)
        for k in range(both):
            attended[:, (h + k) * HD : (h + k + 1) * HD] = done[k]

    each(lambda o: slot_copy(o).wait_send())
    each(lambda o: one_copy(o).wait_send())
    each(lambda o: two_copy(o).wait_send())
    each(lambda o: page_copy(o).wait_send())
    paired(hidden, hid_other, 0).wait_send()
    paired(combined.at[other], recvc, 1).wait_send()


def shards(
    hidden,
    value_weight,
    adapter_down,
    adapter_up,
    block_adapter,
    queries,
    new_keys,
    kv_pool,
    page_request,
    page_pos,
    token_request,
    token_pos,
    send_page,
    send_dest,
    dest_slot,
    send_count,
):
    inst = lax.axis_size("inst")
    tokens, feats = hidden.shape
    rank, wide = adapter_down.shape
    kv_cols = value_weight.shape[1]
    vals = new_keys.shape[1]
    groups = vals // HD
    heads = queries.shape[1] // HD
    pages, page_tokens, page_cols = kv_pool.shape
    keys = pages * page_tokens
    tiles = (rank // 16) * (wide + kv_cols) // HD
    slots = -(-tiles // inst)
    last = inst * page_tokens + tokens
    zero_p = jnp.zeros((6, pages), jnp.int32)
    page_info = jnp.concatenate([page_request[None], page_pos[None], zero_p], axis=0)
    zero_t = jnp.zeros((6, tokens), jnp.int32)
    token_info = jnp.concatenate([token_request[None], token_pos[None], zero_t], axis=0)
    smem = pl.BlockSpec(memory_space=pltpu.SMEM)
    vmem = pl.BlockSpec(memory_space=pltpu.VMEM)
    share = (inst, slots * 16, HD)
    out = pl.pallas_call(
        functools.partial(kernel, inst),
        out_shape=(
            jax.ShapeDtypeStruct((tokens, heads * HD), BF16),
            jax.ShapeDtypeStruct((tokens, vals), BF16),
        ),
        in_specs=[smem] * 5 + [vmem] * 9,
        out_specs=(vmem, vmem),
        scratch_shapes=[
            pltpu.VMEM(share, BF16),
            pltpu.VMEM(share, BF16),
            pltpu.VMEM(share, BF16),
            pltpu.VMEM(share, BF16),
            pltpu.VMEM((inst, page_tokens, page_cols), BF16),
            pltpu.VMEM((inst, page_tokens, page_cols), BF16),
            pltpu.VMEM((inst, 8, HD), jnp.int32),
            pltpu.VMEM((inst, 8, HD), jnp.int32),
            pltpu.VMEM((tokens, feats), BF16),
            pltpu.VMEM((2, rank, feats), BF16),
            pltpu.VMEM((rank, kv_cols), BF16),
            pltpu.VMEM((2, tokens, vals), F32),
            pltpu.VMEM((tokens, vals), F32),
            pltpu.VMEM((heads, tokens, HD), BF16),
            pltpu.VMEM((groups, keys, 2 * HD), BF16),
            pltpu.VMEM((tokens, keys), F32),
            pltpu.VMEM((tokens, last), F32),
            pltpu.VMEM((groups, last, HD), BF16),
            pltpu.VMEM((groups, last, 2 * HD), BF16),
            pltpu.VMEM((heads, tokens, 2 * HD), F32),
            pltpu.VMEM((heads, tokens, HD), F32),
        ]
        + [pltpu.SemaphoreType.DMA((inst,))] * 8
        + [pltpu.SemaphoreType.DMA((2,))] * 2,
        compiler_params=pltpu.CompilerParams(
            collective_id=0, has_side_effects=True, vmem_limit_bytes=56 * 1024 * 1024
        ),
        name="serve",
    )(
        block_adapter,
        send_page,
        send_dest,
        dest_slot,
        send_count,
        page_info,
        token_info,
        hidden,
        value_weight,
        adapter_down,
        adapter_up,
        queries,
        new_keys,
        kv_pool,
    )
    return out


def solution(mesh):
    placed = (
        P(("groups", "inst"), "tensor"),
        P("tensor", None),
        P(("groups", "inst", "tensor"), None),
        P(("groups", "inst", "tensor"), None),
        P("groups"),
        P(("groups", "inst"), "tensor"),
        P(("groups", "inst"), "tensor"),
        P(("groups", "inst"), None, "tensor"),
        P(("groups", "inst")),
        P(("groups", "inst")),
        P(("groups", "inst")),
        P(("groups", "inst")),
        P(("groups", "inst")),
        P(("groups", "inst")),
        P(("groups", "inst")),
        P(("groups", "inst")),
    )
    return jax.shard_map(
        shards,
        mesh=mesh,
        in_specs=placed,
        out_specs=(P(("groups", "inst"), "tensor"), P(("groups", "inst"), "tensor")),
        check_vma=False,
    )
```

```python
import functools
import math

import jax
import jax.numpy as jnp
from jax import lax
from jax.experimental import pallas as pl
from jax.experimental.pallas import tpu as pltpu
from jax.sharding import PartitionSpec as P

HD = 128
FAR = -1e30
FIRST = 3
SECOND = 6
F32 = jnp.float32
BF16 = jnp.bfloat16
MESH = pl.DeviceIdType.MESH


def dot(a, b):
    return jnp.dot(a, b, preferred_element_type=F32)


def dot_t(a, b):
    return lax.dot_general(a, b, (((1,), (1,)), ((), ())), preferred_element_type=F32)


def kernel(
    inst,
    *refs,
):
    sources, refs = refs[:16], refs[16:]
    attended, new_values, refs = refs[0], refs[1], refs[2:]
    places, refs = refs[:16], refs[16:]
    run(inst, sources, attended, new_values, *places, *refs)


def run(
    inst,
    sources,
    attended,
    new_values,
    hidden,
    weight,
    down,
    up,
    block_adapter,
    queries,
    new_keys,
    pool,
    page_request,
    page_pos,
    token_request,
    token_pos,
    send_page,
    send_dest,
    dest_slot,
    send_count,
    stage1,
    recv1,
    stage2,
    recv2,
    out_pages,
    in_pages,
    out_slots,
    in_slots,
    hid_other,
    down_f,
    up_f,
    combined,
    recvc,
    q3,
    vaug,
    bias,
    bias2,
    spread,
    k2,
    v2,
    acc,
    top,
    one_send,
    one_recv,
    two_send,
    two_recv,
    page_send,
    page_recv,
    slot_send,
    slot_recv,
    pair_send,
    pair_recv,
    local_sem,
):
    me = lax.axis_index("inst")
    t = lax.axis_index("tensor")
    other = 1 - t
    tokens = hidden.shape[0]
    feats = hidden.shape[1]
    rank = down.shape[0]
    pages, page_tokens, _ = pool.shape
    keys = pages * page_tokens
    heads = q3.shape[0]
    groups = new_keys.shape[1] // HD
    per = heads // groups
    vals = groups * HD
    mig = send_page.shape[0]
    slots = stage1.shape[1] // 16
    c = math.log2(math.e) / math.sqrt(HD)

    def peer(o):
        return lax.rem(me + o, inst)

    def source(o):
        return lax.rem(me - o + inst, inst)

    def each(body):
        lax.fori_loop(1, inst, lambda o, _: (body(o), 0)[1], 0)

    barrier = pltpu.get_barrier_semaphore()
    each(
        lambda o: pl.semaphore_signal(
            barrier, inc=1, device_id={"inst": peer(o)}, device_id_type=MESH
        )
    )
    pl.semaphore_signal(barrier, inc=1, device_id={"tensor": other}, device_id_type=MESH)

    order = [12, 13, 14, 15, 8, 9, 10, 11, 4, 2, 3, 7, 0, 1, 5, 6]
    mine = (
        hidden,
        weight,
        down,
        up,
        block_adapter,
        queries,
        new_keys,
        pool,
        page_request,
        page_pos,
        token_request,
        token_pos,
        send_page,
        send_dest,
        dest_slot,
        send_count,
    )
    loads = [pltpu.make_async_copy(a, b, local_sem.at[k]) for k, (a, b) in enumerate(zip(sources, mine))]
    for k in order:
        loads[k].start()

    def remote(src, dst, send, recv, o):
        return pltpu.make_async_remote_copy(
            src_ref=src,
            dst_ref=dst,
            send_sem=send.at[o],
            recv_sem=recv.at[o],
            device_id={"inst": peer(o)},
            device_id_type=MESH,
        )

    def paired(src, dst, k):
        return pltpu.make_async_remote_copy(
            src_ref=src,
            dst_ref=dst,
            send_sem=pair_send.at[k],
            recv_sem=pair_recv.at[k],
            device_id={"tensor": other},
            device_id_type=MESH,
        )

    slot_copy = lambda o: remote(out_slots.at[peer(o)], in_slots.at[me], slot_send, slot_recv, o)
    slot_in = lambda o: remote(
        out_slots.at[peer(o)], in_slots.at[source(o)], slot_send, slot_recv, o
    )
    page_copy = lambda o: remote(out_pages.at[peer(o)], in_pages.at[me], page_send, page_recv, o)
    page_in = lambda o: remote(
        out_pages.at[peer(o)], in_pages.at[source(o)], page_send, page_recv, o
    )
    one_copy = lambda o: remote(stage1.at[peer(o)], recv1.at[me], one_send, one_recv, o)
    one_in = lambda o: remote(stage1.at[peer(o)], recv1.at[source(o)], one_send, one_recv, o)
    two_copy = lambda o: remote(stage2.at[peer(o)], recv2.at[me], two_send, two_recv, o)
    two_in = lambda o: remote(stage2.at[peer(o)], recv2.at[source(o)], two_send, two_recv, o)

    loads[2].wait()
    loads[3].wait()
    cols = down.shape[1] // HD
    tiles = []
    for h in range(rank // 16):
        for k in range(cols):
            tiles.append((down, h, k))
    for h in range(rank // 16):
        for k in range(up.shape[1] // HD):
            tiles.append((up, h, k))
    for q, (ref, h, k) in enumerate(tiles):
        at = (q % slots) * 16
        stage1[q // slots, at : at + 16, :] = ref[h * 16 : h * 16 + 16, k * HD : (k + 1) * HD]
    for q in range(len(tiles), inst * slots):
        at = (q % slots) * 16
        stage1[q // slots, at : at + 16, :] = jnp.zeros((16, HD), BF16)

    for k in (12, 13, 14, 15, 7):
        loads[k].wait()
    count = send_count[0]

    def choose(j, _):
        def look(k, found):
            page, slot = found
            hit = (send_dest[k] == j) & (k < count)
            return jnp.where(hit, send_page[k], page), jnp.where(hit, dest_slot[k], slot)

        page, slot = lax.fori_loop(
            0, mig, look, (jnp.int32(0), jnp.int32(-1)), unroll=mig <= 8
        )
        out_slots[j] = jnp.full(out_slots.shape[1:], slot, jnp.int32)
        out_pages[j] = pool[page]
        return 0

    lax.fori_loop(0, inst, choose, 0)

    recv1[me] = stage1[me]
    in_slots[me] = jnp.full(in_slots.shape[1:], -1, jnp.int32)
    in_pages[me] = jnp.zeros(in_pages.shape[1:], BF16)
    for k in (8, 9, 10, 11, 4, 0):
        loads[k].wait()

    t_reqs = token_request[...].astype(F32).reshape(1, tokens)
    t_poss = token_pos[...].astype(F32).reshape(1, tokens)
    t_req = jnp.broadcast_to(t_reqs, (tokens, tokens)).T[:, 0:1]
    t_pos = jnp.broadcast_to(t_poss, (tokens, tokens)).T[:, 0:1]
    ok = (t_reqs == t_req) & (t_poss <= t_pos)
    bias2[:, inst * page_tokens :] = jnp.where(ok, 0.0, FAR)
    owners = jnp.broadcast_to(page_request[...].astype(F32).reshape(1, pages), (8, pages))
    indices = jnp.broadcast_to(page_pos[...].astype(F32).reshape(1, pages), (8, pages))
    owners = owners.astype(BF16)
    indices = indices.astype(BF16)
    spread_page = lax.broadcasted_iota(jnp.int32, (pages, keys), 0)
    spread_key = lax.broadcasted_iota(jnp.int32, (pages, keys), 1) // page_tokens
    spread[...] = (spread_page == spread_key).astype(F32).astype(BF16)
    entry = lax.broadcasted_iota(jnp.int32, (1, keys), 1) % page_tokens
    key_at = dot(indices, spread[...])[0:1] * page_tokens + entry.astype(F32)
    ok = (dot(owners, spread[...])[0:1] == t_req) & (key_at <= t_pos)
    bias[...] = jnp.where(ok, 0.0, FAR)

    pl.semaphore_wait(barrier, inst)
    each(lambda o: slot_copy(o).start())
    each(lambda o: one_copy(o).start())
    paired(hidden, hid_other, 0).start()

    for k in (1, 5, 6):
        loads[k].wait()
    for h in range(heads):
        q3[h] = queries[:, h * HD : (h + 1) * HD]
    for g in range(groups):
        vaug[g, :, :HD] = pool[:, :, (2 * g + 1) * HD : (2 * g + 2) * HD].reshape(keys, HD)
        vaug[g, :, HD:] = jnp.ones((keys, HD), BF16)
        v2[g, :, HD:] = jnp.ones((v2.shape[1], HD), BF16)
        k2[g, inst * page_tokens :, :] = new_keys[:, g * HD : (g + 1) * HD]
    base = dot(hidden[...], weight[...])
    for h in range(2):
        combined[h] = base[:, h * vals : (h + 1) * vals]

    each(lambda o: slot_in(o).wait_recv())
    lane = lax.broadcasted_iota(jnp.int32, (1, HD), 1)
    page_col = lax.broadcasted_iota(jnp.int32, (pages, HD), 0)
    gone = jnp.zeros((8, pages), F32)
    per_row = HD // page_tokens
    for b in range(inst // per_row):
        row = jnp.full((1, HD), -1, jnp.int32)
        for j in range(per_row):
            row = jnp.where(lane // page_tokens == j, in_slots[b * per_row + j][0:1], row)
        match = (page_col == row).astype(F32).astype(BF16)
        gone = gone + dot_t(jnp.ones((8, HD), BF16), match)
        req = jnp.where(row >= 0, dot(owners, match)[0:1], -2.0)
        at = dot(indices, match)[0:1] * page_tokens + (lane % page_tokens).astype(F32)
        ok = (req == t_req) & (at <= t_pos)
        bias2[:, b * HD : (b + 1) * HD] = jnp.where(ok, 0.0, FAR)
    gone = (gone > 0.5).astype(F32).astype(BF16)
    lost = dot(gone, spread[...])[0:1] > 0.5
    bias[...] = jnp.where(lost, FAR, bias[...])

    both = 2

    def pool_part(lo, hi):
        def step(i, _):
            h = i * both
            g = h // per
            q = q3[pl.ds(h, both)].reshape(both * tokens, HD)
            lanes = pl.ds(pl.multiple_of(g * (2 * HD), 2 * HD), HD)
            n = keys // 512
            scored = []
            m = None
            for j in range(n):
                k = pool[j * 512 // page_tokens : (j + 1) * 512 // page_tokens, :, lanes]
                s = dot_t(q, k.reshape(512, HD)).reshape(both, tokens, 512)
                s = s + bias[:, j * 512 : (j + 1) * 512][None]
                part = jnp.max(s, axis=-1, keepdims=True)
                m = part if m is None else jnp.maximum(m, part)
                scored.append(s)
            total = None
            for j in range(n):
                p = jnp.exp2((scored[j] - m) * c).astype(BF16).reshape(both * tokens, 512)
                part = dot(p, vaug[g, j * 512 : (j + 1) * 512])
                total = part if total is None else total + part
            acc[pl.ds(h, both)] = total.reshape(both, tokens, 2 * HD)
            top[pl.ds(h, both)] = jnp.broadcast_to(m, (both, tokens, HD))
            return 0

        lax.fori_loop(lo, hi, step, 0)

    steps = heads // both
    pool_part(0, FIRST)
    each(lambda o: one_in(o).wait_recv())

    def pick(j, _):
        stage2[j] = recv1[block_adapter[j]]
        return 0

    lax.fori_loop(0, inst, pick, 0)
    each(lambda o: two_copy(o).start())
    each(lambda o: page_copy(o).start())
    recv2[me] = stage2[me]
    pool_part(FIRST, SECOND)

    each(lambda o: two_in(o).wait_recv())
    paired(hidden, hid_other, 0).wait_recv()
    for q, (ref, h, k) in enumerate(tiles):
        at = (q % slots) * 16
        tile = recv2[q // slots, at : at + 16, :]
        if ref is down:
            side, col = divmod(k * HD, feats)
            down_f[side, h * 16 : h * 16 + 16, col : col + HD] = tile
        else:
            up_f[h * 16 : h * 16 + 16, k * HD : (k + 1) * HD] = tile
    low = dot_t(hidden[...], down_f[t]) + dot_t(hid_other[...], down_f[other])
    delta = jnp.zeros((tokens, up.shape[1]), F32)
    for _ in range(3):
        part = low.astype(BF16)
        low = low - part.astype(F32)
        delta = delta + dot(part, up_f[...])
    for h in range(2):
        combined[h] = combined[h] + delta[:, h * vals : (h + 1) * vals]
    paired(combined.at[other], recvc, 1).start()

    pool_part(SECOND, steps)

    paired(combined.at[other], recvc, 1).wait_recv()
    each(lambda o: page_in(o).wait_recv())
    values = (combined[t] + recvc[...]).astype(BF16)
    new_values[...] = values
    arrived = inst * page_tokens
    for g in range(groups):
        k2[g, :arrived, :] = in_pages[:, :, 2 * g * HD : (2 * g + 1) * HD].reshape(arrived, HD)
        v2[g, :arrived, :HD] = in_pages[:, :, (2 * g + 1) * HD : (2 * g + 2) * HD].reshape(
            arrived, HD
        )
        v2[g, arrived:, :HD] = values[:, g * HD : (g + 1) * HD]
    for h in range(0, heads, both):
        g = h // per
        q = q3[h : h + both].reshape(both * tokens, HD)
        s = dot_t(q, k2[g]).reshape(both, tokens, k2.shape[1]) + bias2[...][None]
        m_old = top[h : h + both][:, :, 0:1]
        m = jnp.maximum(jnp.max(s, axis=-1, keepdims=True), m_old)
        p = jnp.exp2((s - m) * c).astype(BF16).reshape(both * tokens, k2.shape[1])
        keep = jnp.exp2((m_old - m) * c)
        whole = acc[h : h + both] * keep + dot(p, v2[g]).reshape(both, tokens, 2 * HD)
        done = (whole[:, :, :HD] / whole[:, :, HD:]).astype(BF16)
        for k in range(both):
            attended[:, (h + k) * HD : (h + k + 1) * HD] = done[k]

    each(lambda o: slot_copy(o).wait_send())
    each(lambda o: one_copy(o).wait_send())
    each(lambda o: two_copy(o).wait_send())
    each(lambda o: page_copy(o).wait_send())
    paired(hidden, hid_other, 0).wait_send()
    paired(combined.at[other], recvc, 1).wait_send()


def settle(attended, new_values, attended_out, new_values_out):
    attended_out[...] = attended[...]
    new_values_out[...] = new_values[...]


def shards(*args):
    hidden, value_weight, adapter_down = args[:3]
    queries, new_keys, kv_pool = args[5:8]
    inst = lax.axis_size("inst")
    tokens, feats = hidden.shape
    rank, wide = adapter_down.shape
    kv_cols = value_weight.shape[1]
    vals = new_keys.shape[1]
    groups = vals // HD
    heads = queries.shape[1] // HD
    pages, page_tokens, page_cols = kv_pool.shape
    keys = pages * page_tokens
    tiles = (rank // 16) * (wide + kv_cols) // HD
    slots = -(-tiles // inst)
    last = inst * page_tokens + tokens
    anywhere = pl.BlockSpec(memory_space=pl.ANY)
    vmem = pl.BlockSpec(memory_space=pltpu.VMEM)
    share = (inst, slots * 16, HD)
    out = pl.pallas_call(
        functools.partial(kernel, inst),
        out_shape=(
            jax.ShapeDtypeStruct((tokens, heads * HD), BF16),
            jax.ShapeDtypeStruct((tokens, vals), BF16),
        ),
        in_specs=[anywhere] * 16,
        out_specs=(vmem, vmem),
        scratch_shapes=[
            (pltpu.SMEM if k in (4, 12, 13, 14, 15) else pltpu.VMEM)(a.shape, a.dtype)
            for k, a in enumerate(args)
        ]
        + [
            pltpu.VMEM(share, BF16),
            pltpu.VMEM(share, BF16),
            pltpu.VMEM(share, BF16),
            pltpu.VMEM(share, BF16),
            pltpu.VMEM((inst, page_tokens, page_cols), BF16),
            pltpu.VMEM((inst, page_tokens, page_cols), BF16),
            pltpu.VMEM((inst, 8, HD), jnp.int32),
            pltpu.VMEM((inst, 8, HD), jnp.int32),
            pltpu.VMEM((tokens, feats), BF16),
            pltpu.VMEM((2, rank, feats), BF16),
            pltpu.VMEM((rank, kv_cols), BF16),
            pltpu.VMEM((2, tokens, vals), F32),
            pltpu.VMEM((tokens, vals), F32),
            pltpu.VMEM((heads, tokens, HD), BF16),
            pltpu.VMEM((groups, keys, 2 * HD), BF16),
            pltpu.VMEM((tokens, keys), F32),
            pltpu.VMEM((tokens, last), F32),
            pltpu.VMEM((pages, keys), BF16),
            pltpu.VMEM((groups, last, HD), BF16),
            pltpu.VMEM((groups, last, 2 * HD), BF16),
            pltpu.VMEM((heads, tokens, 2 * HD), F32),
            pltpu.VMEM((heads, tokens, HD), F32),
        ]
        + [pltpu.SemaphoreType.DMA((inst,))] * 8
        + [pltpu.SemaphoreType.DMA((2,))] * 2
        + [pltpu.SemaphoreType.DMA((16,))],
        compiler_params=pltpu.CompilerParams(
            collective_id=0, has_side_effects=True, vmem_limit_bytes=56 * 1024 * 1024
        ),
        name="serve",
    )(
        *args
    )
    return pl.pallas_call(
        settle,
        out_shape=tuple(jax.ShapeDtypeStruct(a.shape, a.dtype) for a in out),
        in_specs=[vmem] * 2,
        out_specs=(vmem, vmem),
        name="settle",
    )(*out)


def solution(mesh):
    placed = (
        P(("groups", "inst"), "tensor"),
        P("tensor", None),
        P(("groups", "inst", "tensor"), None),
        P(("groups", "inst", "tensor"), None),
        P("groups"),
        P(("groups", "inst"), "tensor"),
        P(("groups", "inst"), "tensor"),
        P(("groups", "inst"), None, "tensor"),
        P(("groups", "inst")),
        P(("groups", "inst")),
        P(("groups", "inst")),
        P(("groups", "inst")),
        P(("groups", "inst")),
        P(("groups", "inst")),
        P(("groups", "inst")),
        P(("groups", "inst")),
    )
    return jax.shard_map(
        shards,
        mesh=mesh,
        in_specs=placed,
        out_specs=(P(("groups", "inst"), "tensor"), P(("groups", "inst"), "tensor")),
        check_vma=False,
    )
```

```python
import functools
import math

import jax
import jax.numpy as jnp
from jax import lax
from jax.experimental import pallas as pl
from jax.experimental.pallas import tpu as pltpu
from jax.sharding import PartitionSpec as P

HD = 128
FAR = -1e30
FIRST = 1
SECOND = 3
F32 = jnp.float32
BF16 = jnp.bfloat16
MESH = pl.DeviceIdType.MESH


def dot(a, b):
    return jnp.dot(a, b, preferred_element_type=F32)


def dot_t(a, b):
    return lax.dot_general(a, b, (((1,), (1,)), ((), ())), preferred_element_type=F32)


def kernel(
    inst,
    *refs,
):
    sources, refs = refs[:16], refs[16:]
    attended, new_values, refs = refs[0], refs[1], refs[2:]
    places, refs = refs[:16], refs[16:]
    run(inst, sources, attended, new_values, *places, *refs)


def run(
    inst,
    sources,
    attended,
    new_values,
    hidden,
    weight,
    down,
    up,
    block_adapter,
    queries,
    new_keys,
    pool,
    page_request,
    page_pos,
    token_request,
    token_pos,
    send_page,
    send_dest,
    dest_slot,
    send_count,
    stage1,
    recv1,
    stage2,
    recv2,
    out_pages,
    in_pages,
    out_slots,
    in_slots,
    hid_other,
    down_f,
    up_f,
    combined,
    recvc,
    q3,
    vaug,
    bias,
    bias2,
    spread,
    k2,
    v2,
    acc,
    top,
    one_send,
    one_recv,
    two_send,
    two_recv,
    page_send,
    page_recv,
    slot_send,
    slot_recv,
    pair_send,
    pair_recv,
    local_sem,
):
    me = lax.axis_index("inst")
    t = lax.axis_index("tensor")
    other = 1 - t
    tokens = hidden.shape[0]
    feats = hidden.shape[1]
    rank = down.shape[0]
    pages, page_tokens, _ = pool.shape
    keys = pages * page_tokens
    heads = q3.shape[0]
    groups = new_keys.shape[1] // HD
    per = heads // groups
    vals = groups * HD
    mig = send_page.shape[0]
    slots = stage1.shape[1] // 16
    c = math.log2(math.e) / math.sqrt(HD)

    def peer(o):
        return lax.rem(me + o, inst)

    def source(o):
        return lax.rem(me - o + inst, inst)

    def each(body):
        lax.fori_loop(1, inst, lambda o, _: (body(o), 0)[1], 0)

    barrier = pltpu.get_barrier_semaphore()
    each(
        lambda o: pl.semaphore_signal(
            barrier, inc=1, device_id={"inst": peer(o)}, device_id_type=MESH
        )
    )
    pl.semaphore_signal(barrier, inc=1, device_id={"tensor": other}, device_id_type=MESH)

    order = [12, 13, 14, 15, 8, 9, 10, 11, 4, 2, 3, 7, 0, 1, 5, 6]
    mine = (
        hidden,
        weight,
        down,
        up,
        block_adapter,
        queries,
        new_keys,
        pool,
        page_request,
        page_pos,
        token_request,
        token_pos,
        send_page,
        send_dest,
        dest_slot,
        send_count,
    )
    loads = [pltpu.make_async_copy(a, b, local_sem.at[k]) for k, (a, b) in enumerate(zip(sources, mine))]
    for k in order:
        loads[k].start()

    def remote(src, dst, send, recv, o):
        return pltpu.make_async_remote_copy(
            src_ref=src,
            dst_ref=dst,
            send_sem=send.at[o],
            recv_sem=recv.at[o],
            device_id={"inst": peer(o)},
            device_id_type=MESH,
        )

    def paired(src, dst, k):
        return pltpu.make_async_remote_copy(
            src_ref=src,
            dst_ref=dst,
            send_sem=pair_send.at[k],
            recv_sem=pair_recv.at[k],
            device_id={"tensor": other},
            device_id_type=MESH,
        )

    slot_copy = lambda o: remote(out_slots.at[peer(o)], in_slots.at[me], slot_send, slot_recv, o)
    slot_in = lambda o: remote(
        out_slots.at[peer(o)], in_slots.at[source(o)], slot_send, slot_recv, o
    )
    page_copy = lambda o: remote(out_pages.at[peer(o)], in_pages.at[me], page_send, page_recv, o)
    page_in = lambda o: remote(
        out_pages.at[peer(o)], in_pages.at[source(o)], page_send, page_recv, o
    )
    one_copy = lambda o: remote(stage1.at[peer(o)], recv1.at[me], one_send, one_recv, o)
    one_in = lambda o: remote(stage1.at[peer(o)], recv1.at[source(o)], one_send, one_recv, o)
    two_copy = lambda o: remote(stage2.at[peer(o)], recv2.at[me], two_send, two_recv, o)
    two_in = lambda o: remote(stage2.at[peer(o)], recv2.at[source(o)], two_send, two_recv, o)

    loads[2].wait()
    loads[3].wait()
    cols = down.shape[1] // HD
    tiles = []
    for h in range(rank // 16):
        for k in range(cols):
            tiles.append((down, h, k))
    for h in range(rank // 16):
        for k in range(up.shape[1] // HD):
            tiles.append((up, h, k))
    for q, (ref, h, k) in enumerate(tiles):
        at = (q % slots) * 16
        stage1[q // slots, at : at + 16, :] = ref[h * 16 : h * 16 + 16, k * HD : (k + 1) * HD]
    for q in range(len(tiles), inst * slots):
        at = (q % slots) * 16
        stage1[q // slots, at : at + 16, :] = jnp.zeros((16, HD), BF16)

    for k in (12, 13, 14, 15, 7):
        loads[k].wait()
    count = send_count[0]

    def choose(j, _):
        def look(k, found):
            page, slot = found
            hit = (send_dest[k] == j) & (k < count)
            return jnp.where(hit, send_page[k], page), jnp.where(hit, dest_slot[k], slot)

        page, slot = lax.fori_loop(
            0, mig, look, (jnp.int32(0), jnp.int32(-1)), unroll=mig <= 8
        )
        out_slots[j] = jnp.full(out_slots.shape[1:], slot, jnp.int32)
        out_pages[j] = pool[page]
        return 0

    lax.fori_loop(0, inst, choose, 0)

    recv1[me] = stage1[me]
    in_slots[me] = jnp.full(in_slots.shape[1:], -1, jnp.int32)
    in_pages[me] = jnp.zeros(in_pages.shape[1:], BF16)
    for k in (8, 9, 10, 11, 4, 0):
        loads[k].wait()

    t_reqs = token_request[...].astype(F32).reshape(1, tokens)
    t_poss = token_pos[...].astype(F32).reshape(1, tokens)
    t_req = jnp.broadcast_to(t_reqs, (tokens, tokens)).T[:, 0:1]
    t_pos = jnp.broadcast_to(t_poss, (tokens, tokens)).T[:, 0:1]
    ok = (t_reqs == t_req) & (t_poss <= t_pos)
    bias2[:, inst * page_tokens :] = jnp.where(ok, 0.0, FAR)
    owners = jnp.broadcast_to(page_request[...].astype(F32).reshape(1, pages), (8, pages))
    indices = jnp.broadcast_to(page_pos[...].astype(F32).reshape(1, pages), (8, pages))
    owners = owners.astype(BF16)
    indices = indices.astype(BF16)
    spread_page = lax.broadcasted_iota(jnp.int32, (pages, keys), 0)
    spread_key = lax.broadcasted_iota(jnp.int32, (pages, keys), 1)
    inside = spread_key - spread_page * page_tokens
    spread[...] = ((inside >= 0) & (inside < page_tokens)).astype(F32).astype(BF16)
    entry = lax.broadcasted_iota(jnp.int32, (1, keys), 1) & (page_tokens - 1)
    key_at = dot(indices, spread[...])[0:1] * page_tokens + entry.astype(F32)
    ok = (dot(owners, spread[...])[0:1] == t_req) & (key_at <= t_pos)
    bias[...] = jnp.where(ok, 0.0, FAR)

    pl.semaphore_wait(barrier, inst)
    each(lambda o: slot_copy(o).start())
    each(lambda o: one_copy(o).start())
    paired(hidden, hid_other, 0).start()

    for k in (1, 5, 6):
        loads[k].wait()
    for h in range(heads):
        q3[h] = queries[:, h * HD : (h + 1) * HD]
    for g in range(groups):
        vaug[g, :, :HD] = pool[:, :, (2 * g + 1) * HD : (2 * g + 2) * HD].reshape(keys, HD)
        vaug[g, :, HD:] = jnp.ones((keys, HD), BF16)
        v2[g, :, HD:] = jnp.ones((v2.shape[1], HD), BF16)
        k2[g, inst * page_tokens :, :] = new_keys[:, g * HD : (g + 1) * HD]
    base = dot(hidden[...], weight[...])
    for h in range(2):
        combined[h] = base[:, h * vals : (h + 1) * vals]

    each(lambda o: slot_in(o).wait_recv())
    lane = lax.broadcasted_iota(jnp.int32, (1, HD), 1)
    page_col = lax.broadcasted_iota(jnp.int32, (pages, HD), 0)
    gone = jnp.zeros((8, pages), F32)
    per_row = HD // page_tokens
    for b in range(inst // per_row):
        row = jnp.full((1, HD), -1, jnp.int32)
        for j in range(per_row):
            row = jnp.where((lane >= j * page_tokens) & (lane < (j + 1) * page_tokens), in_slots[b * per_row + j][0:1], row)
        match = (page_col == row).astype(F32).astype(BF16)
        gone = gone + dot_t(jnp.ones((8, HD), BF16), match)
        req = jnp.where(row >= 0, dot(owners, match)[0:1], -2.0)
        at = dot(indices, match)[0:1] * page_tokens + (lane & (page_tokens - 1)).astype(F32)
        ok = (req == t_req) & (at <= t_pos)
        bias2[:, b * HD : (b + 1) * HD] = jnp.where(ok, 0.0, FAR)
    gone = (gone > 0.5).astype(F32).astype(BF16)
    lost = dot(gone, spread[...])[0:1] > 0.5
    bias[...] = jnp.where(lost, FAR, bias[...])

    both = 4

    def pool_part(lo, hi):
        def step(i, _):
            h = i * both
            g = h // per
            q = q3[pl.ds(h, both)].reshape(both * tokens, HD)
            lanes = pl.ds(pl.multiple_of(g * (2 * HD), 2 * HD), HD)
            n = keys // 512
            scored = []
            m = None
            for j in range(n):
                k = pool[j * 512 // page_tokens : (j + 1) * 512 // page_tokens, :, lanes]
                s = dot_t(q, k.reshape(512, HD)).reshape(both, tokens, 512)
                s = s + bias[:, j * 512 : (j + 1) * 512][None]
                part = jnp.max(s, axis=-1, keepdims=True)
                m = part if m is None else jnp.maximum(m, part)
                scored.append(s)
            total = None
            for j in range(n):
                p = jnp.exp2((scored[j] - m) * c).astype(BF16).reshape(both * tokens, 512)
                part = dot(p, vaug[g, j * 512 : (j + 1) * 512])
                total = part if total is None else total + part
            acc[pl.ds(h, both)] = total.reshape(both, tokens, 2 * HD)
            top[pl.ds(h, both)] = jnp.broadcast_to(m, (both, tokens, HD))
            return 0

        lax.fori_loop(lo, hi, step, 0)

    steps = heads // both
    pool_part(0, FIRST)
    each(lambda o: one_in(o).wait_recv())

    def pick(j, _):
        stage2[j] = recv1[block_adapter[j]]
        return 0

    lax.fori_loop(0, inst, pick, 0)
    each(lambda o: two_copy(o).start())
    each(lambda o: page_copy(o).start())
    recv2[me] = stage2[me]
    pool_part(FIRST, SECOND)

    each(lambda o: two_in(o).wait_recv())
    paired(hidden, hid_other, 0).wait_recv()
    for q, (ref, h, k) in enumerate(tiles):
        at = (q % slots) * 16
        tile = recv2[q // slots, at : at + 16, :]
        if ref is down:
            side, col = divmod(k * HD, feats)
            down_f[side, h * 16 : h * 16 + 16, col : col + HD] = tile
        else:
            up_f[h * 16 : h * 16 + 16, k * HD : (k + 1) * HD] = tile
    low = dot_t(hidden[...], down_f[t]) + dot_t(hid_other[...], down_f[other])
    delta = jnp.zeros((tokens, up.shape[1]), F32)
    for _ in range(3):
        part = low.astype(BF16)
        low = low - part.astype(F32)
        delta = delta + dot(part, up_f[...])
    for h in range(2):
        combined[h] = combined[h] + delta[:, h * vals : (h + 1) * vals]
    paired(combined.at[other], recvc, 1).start()

    pool_part(SECOND, steps)

    paired(combined.at[other], recvc, 1).wait_recv()
    each(lambda o: page_in(o).wait_recv())
    values = (combined[t] + recvc[...]).astype(BF16)
    new_values[...] = values
    arrived = inst * page_tokens
    for g in range(groups):
        k2[g, :arrived, :] = in_pages[:, :, 2 * g * HD : (2 * g + 1) * HD].reshape(arrived, HD)
        v2[g, :arrived, :HD] = in_pages[:, :, (2 * g + 1) * HD : (2 * g + 2) * HD].reshape(
            arrived, HD
        )
        v2[g, arrived:, :HD] = values[:, g * HD : (g + 1) * HD]
    for h in range(0, heads, both):
        g = h // per
        q = q3[h : h + both].reshape(both * tokens, HD)
        s = dot_t(q, k2[g]).reshape(both, tokens, k2.shape[1]) + bias2[...][None]
        m_old = top[h : h + both][:, :, 0:1]
        m = jnp.maximum(jnp.max(s, axis=-1, keepdims=True), m_old)
        p = jnp.exp2((s - m) * c).astype(BF16).reshape(both * tokens, k2.shape[1])
        keep = jnp.exp2((m_old - m) * c)
        whole = acc[h : h + both] * keep + dot(p, v2[g]).reshape(both, tokens, 2 * HD)
        done = (whole[:, :, :HD] / whole[:, :, HD:]).astype(BF16)
        for k in range(both):
            attended[:, (h + k) * HD : (h + k + 1) * HD] = done[k]

    each(lambda o: slot_copy(o).wait_send())
    each(lambda o: one_copy(o).wait_send())
    each(lambda o: two_copy(o).wait_send())
    each(lambda o: page_copy(o).wait_send())
    paired(hidden, hid_other, 0).wait_send()
    paired(combined.at[other], recvc, 1).wait_send()


def settle(attended, new_values, attended_out, new_values_out):
    attended_out[...] = attended[...]
    new_values_out[...] = new_values[...]


def shards(*args):
    hidden, value_weight, adapter_down = args[:3]
    queries, new_keys, kv_pool = args[5:8]
    inst = lax.axis_size("inst")
    tokens, feats = hidden.shape
    rank, wide = adapter_down.shape
    kv_cols = value_weight.shape[1]
    vals = new_keys.shape[1]
    groups = vals // HD
    heads = queries.shape[1] // HD
    pages, page_tokens, page_cols = kv_pool.shape
    keys = pages * page_tokens
    tiles = (rank // 16) * (wide + kv_cols) // HD
    slots = -(-tiles // inst)
    last = inst * page_tokens + tokens
    anywhere = pl.BlockSpec(memory_space=pl.ANY)
    vmem = pl.BlockSpec(memory_space=pltpu.VMEM)
    share = (inst, slots * 16, HD)
    out = pl.pallas_call(
        functools.partial(kernel, inst),
        out_shape=(
            jax.ShapeDtypeStruct((tokens, heads * HD), BF16),
            jax.ShapeDtypeStruct((tokens, vals), BF16),
        ),
        in_specs=[anywhere] * 16,
        out_specs=(vmem, vmem),
        scratch_shapes=[
            (pltpu.SMEM if k in (4, 12, 13, 14, 15) else pltpu.VMEM)(a.shape, a.dtype)
            for k, a in enumerate(args)
        ]
        + [
            pltpu.VMEM(share, BF16),
            pltpu.VMEM(share, BF16),
            pltpu.VMEM(share, BF16),
            pltpu.VMEM(share, BF16),
            pltpu.VMEM((inst, page_tokens, page_cols), BF16),
            pltpu.VMEM((inst, page_tokens, page_cols), BF16),
            pltpu.VMEM((inst, 8, HD), jnp.int32),
            pltpu.VMEM((inst, 8, HD), jnp.int32),
            pltpu.VMEM((tokens, feats), BF16),
            pltpu.VMEM((2, rank, feats), BF16),
            pltpu.VMEM((rank, kv_cols), BF16),
            pltpu.VMEM((2, tokens, vals), F32),
            pltpu.VMEM((tokens, vals), F32),
            pltpu.VMEM((heads, tokens, HD), BF16),
            pltpu.VMEM((groups, keys, 2 * HD), BF16),
            pltpu.VMEM((tokens, keys), F32),
            pltpu.VMEM((tokens, last), F32),
            pltpu.VMEM((pages, keys), BF16),
            pltpu.VMEM((groups, last, HD), BF16),
            pltpu.VMEM((groups, last, 2 * HD), BF16),
            pltpu.VMEM((heads, tokens, 2 * HD), F32),
            pltpu.VMEM((heads, tokens, HD), F32),
        ]
        + [pltpu.SemaphoreType.DMA((inst,))] * 8
        + [pltpu.SemaphoreType.DMA((2,))] * 2
        + [pltpu.SemaphoreType.DMA((16,))],
        compiler_params=pltpu.CompilerParams(
            collective_id=0, has_side_effects=True, vmem_limit_bytes=56 * 1024 * 1024
        ),
        name="serve",
    )(
        *args
    )
    return pl.pallas_call(
        settle,
        out_shape=tuple(jax.ShapeDtypeStruct(a.shape, a.dtype) for a in out),
        in_specs=[vmem] * 2,
        out_specs=(vmem, vmem),
        name="settle",
    )(*out)


def solution(mesh):
    placed = (
        P(("groups", "inst"), "tensor"),
        P("tensor", None),
        P(("groups", "inst", "tensor"), None),
        P(("groups", "inst", "tensor"), None),
        P("groups"),
        P(("groups", "inst"), "tensor"),
        P(("groups", "inst"), "tensor"),
        P(("groups", "inst"), None, "tensor"),
        P(("groups", "inst")),
        P(("groups", "inst")),
        P(("groups", "inst")),
        P(("groups", "inst")),
        P(("groups", "inst")),
        P(("groups", "inst")),
        P(("groups", "inst")),
        P(("groups", "inst")),
    )
    return jax.shard_map(
        shards,
        mesh=mesh,
        in_specs=placed,
        out_specs=(P(("groups", "inst"), "tensor"), P(("groups", "inst"), "tensor")),
        check_vma=False,
    )
```
